32 devices in a mesh: dp: 4 (over x, core), tensor: 8 (over z, y).
Axes of the slice: x: 2, y: 2, z: 4, core: 2. Of those that a mesh axis runs over, the one named last changes fastest.
Arguments:
- hidden: bfloat16 [768, 14336], P('dp', 'tensor'), parts along dimension 0, may hold values from -6 to 6
- down_weight: bfloat16 [14336, 8192], P('tensor'), may hold values from -0.046875 to 0.046875
- residual: bfloat16 [768, 8192], P('dp', 'tensor'), parts along dimension 0, may hold values from -100 to 100
- norm_gain: float32 [8192], replicated, may hold values from 0.1 to 1.9
- qkv_weight: bfloat16 [8192, 5120], P(None, 'tensor'), may hold values from -0.0625 to 0.0625
Outputs:
- stream: bfloat16 [768, 8192], P('dp', 'tensor'), parts along dimension 0
- qkv: bfloat16 [768, 5120], P('dp', 'tensor'), parts along dimension 0
The draws below stay inside these ranges and needn't reach their ends.
There are 4 independent parts, one for each index of `dp`. The reference program is written for one: setup_inputs(seed, part) draws one part's arguments, and reference() takes and returns one part's arrays. A program takes and returns all parts, laid end to end along the dimension named above; an argument that names none is the same for every part. Nothing has to cross between parts.
All inputs are finite; a program needn't handle non-finite values.
Results may differ from the reference program's by a relative error of at most 0.02.
Values may be sent and summed in bfloat16 or wider, within the bound.
No kernel may reach another device: no remote copies, remote signals or barrier semaphores. Data moves between devices by JAX's collectives and lax.ppermute only.
A program may use at most 128 MiB of HBM per device.

```python
import jax
import jax.numpy as jnp
from jax import lax

D = 8192
FF = 14336
QKV = 5120
TOKENS = 192
N_TENSOR = 8


def draw_residual(key, part):
    key_base, key_rows, key_cols = jax.random.split(jax.random.fold_in(key, 7), 3)
    values = jnp.clip(jax.random.normal(key_base, (TOKENS, D), jnp.float32), -4.0, 4.0)
    row_draw = jax.random.uniform(key_rows, (TOKENS, 1), jnp.float32)
    col_draw = jax.random.uniform(key_cols, (1, D), jnp.float32)
    position = jnp.arange(D, dtype=jnp.float32)[None, :] / D
    col_scale = jnp.power(3.0, position - 0.5) * jnp.power(10.0, 0.5 * (col_draw - 0.5))
    row_scale = jnp.power(10.0, row_draw - 0.5)
    return (values * row_scale * col_scale).astype(jnp.bfloat16)


def levels(rng, extent, shards, low, high):
    gain, own = 1.0, jax.random.fold_in(rng, 6)
    for dim, parts in shards:
        draws = jnp.exp(jax.random.uniform(jax.random.fold_in(own, dim), (parts,), jnp.float32, low / len(shards), high / len(shards)))
        gain = gain * jnp.repeat(draws, extent[dim] // parts).reshape([-1 if axis == dim else 1 for axis in range(len(extent))])
    return gain


def scatter_about(key, extent, spread, most, cuts=(), kind=jnp.bfloat16):
    loudness = levels(key, extent, cuts, -0.22, 0.18) if cuts else 1.0
    array = jax.random.normal(key, extent, jnp.float32) * spread * loudness
    return jnp.minimum(jnp.maximum(array, -most), most).astype(kind)


def setup_inputs(seed: int = 0, part: int = 0) -> dict:
    streams_of = jax.random.split(jax.random.key(seed), 6)
    part_splits = jax.random.split(jax.random.fold_in(streams_of[5], part), 6)
    hidden = scatter_about(part_splits[0], (TOKENS, FF), 1.0, 6.0, ((1, 8),))
    down_weight = scatter_about(streams_of[1], (FF, D), FF ** -0.5, 0.046875, ((0, 8),))
    residual = draw_residual(jax.random.fold_in(jax.random.fold_in(streams_of[5], part), 71), part)
    norm_gain = jnp.clip(1.0 + 0.18 * jax.random.normal(streams_of[3], (D,), jnp.float32), 0.1, 1.9)
    qkv_weight = scatter_about(streams_of[4], (D, QKV), D ** -0.5, 0.0625, ((1, 8),))
    return {"hidden": hidden, "down_weight": down_weight, "residual": residual, "norm_gain": norm_gain, "qkv_weight": qkv_weight}


epsilon = 1e-05

def reference(hidden, down_weight, residual, norm_gain, qkv_weight):
    groups = N_TENSOR
    width = FF // groups
    hidden_groups = jnp.transpose(hidden.reshape(TOKENS, groups, width), (1, 0, 2))
    down_groups = down_weight.reshape(groups, width, D)

    def add_group(total, pieces):
        part = jnp.dot(pieces[0], pieces[1], preferred_element_type=jnp.float32)
        part = lax.optimization_barrier(part.astype(jnp.bfloat16))
        return (total + part.astype(jnp.float32), None)
    start_total = jnp.zeros((TOKENS, D), jnp.float32)
    partial_sum, _ = lax.scan(add_group, start_total, (hidden_groups, down_groups))
    summed = partial_sum + residual.astype(jnp.float32)
    stream = summed.astype(jnp.bfloat16)
    scale = jnp.sqrt(lax.optimization_barrier(jnp.mean(summed * summed, axis=1, keepdims=True)) + epsilon)
    normed = (summed / scale * norm_gain[None, :]).astype(jnp.bfloat16)
    qkv = jnp.dot(normed, qkv_weight, preferred_element_type=jnp.float32).astype(jnp.bfloat16)
    return (stream, qkv)
```

```python
import functools

import jax
import jax.numpy as jnp
from jax import lax
from jax.experimental import pallas as pl
from jax.experimental.pallas import tpu as pltpu
from jax.sharding import PartitionSpec as P

epsilon = 1e-05
f32, bf16 = jnp.float32, jnp.bfloat16
MIB = 1024 * 1024


def ring_order(n):
    return list(range(0, n, 2)) + list(range(n - 1, 0, -2))


def owner(n, offset):
    me = lax.axis_index("tensor")
    place = jnp.where(me % 2 == 0, me // 2, n - 1 - me // 2)
    place = (place + (offset + n)) % n
    return jnp.where(place < n // 2, 2 * place, 2 * (n - 1 - place) + 1)


def down_kernel(n, parts, x_ref, w_ref, *rest):
    outs, rest = rest[: len(parts)], list(rest[len(parts) :])
    buf, sems = rest[-2:]
    if len(rest) > 2:
        x_out, x_sem = rest[:2]
        x_copy = pltpu.make_async_copy(x_ref, x_out, x_sem)
        x_copy.start()
    else:
        x_out, x_copy = x_ref, None
    sub = outs[0].shape[1]
    per, (count, pieces) = sub // buf.shape[2], sems.shape
    tile, deep = buf.shape[2], buf.shape[1] // pieces

    def copies(i, begin, j):
        at = i * per + j
        columns = pl.ds(pl.multiple_of(begin + j * tile, tile), tile)
        for p in range(pieces):
            rows = pl.ds(p * deep, deep)
            yield pltpu.make_async_copy(w_ref.at[rows, columns], buf.at[at, rows], sems.at[at, p])

    begins = [owner(n, offset) * (2 * sub) + half * sub for offset, half in parts]
    for i in range(len(parts)):
        for j in range(per):
            for copy in copies(i, begins[i], j):
                copy.start()
    if x_copy is not None:
        x_copy.wait()
    for i, out in enumerate(outs):

        def step(j, carry):
            for copy in copies(i, begins[i], j):
                copy.wait()
            part = jnp.dot(x_out[...], buf[i * per + j], preferred_element_type=f32)
            out[:, pl.ds(pl.multiple_of(j * tile, tile), tile)] = part.astype(bf16)
            return carry

        lax.fori_loop(0, per, step, 0)


def down(n, parts, hidden, down_weight, sub, first=False):
    rows, inner = hidden.shape
    vmem, hbm = pl.BlockSpec(memory_space=pltpu.VMEM), pl.BlockSpec(memory_space=pltpu.HBM)
    pieces = max(p for p in (1, 2, 4) if inner % (16 * p) == 0)
    tile = sub
    count = len(parts) * (sub // tile)
    weight = pltpu.with_memory_space_constraint(down_weight, pltpu.HBM)
    out_shape = [pltpu.VMEM((rows, sub), bf16)] * len(parts)
    scratch = [pltpu.VMEM((count, inner, tile), bf16), pltpu.SemaphoreType.DMA((count, pieces))]
    if first:
        hidden = pltpu.with_memory_space_constraint(hidden, pltpu.HBM)
        out_shape = out_shape + [pltpu.VMEM(hidden.shape, bf16)]
        scratch = [pltpu.SemaphoreType.DMA] + scratch
    return pl.pallas_call(
        functools.partial(down_kernel, n, parts),
        out_shape=out_shape,
        in_specs=[hbm if first else vmem, hbm],
        out_specs=[vmem] * len(out_shape),
        scratch_shapes=scratch,
        compiler_params=pltpu.CompilerParams(vmem_limit_bytes=14 * MIB),
        cost_estimate=pl.CostEstimate(
            flops=2 * rows * inner * sub * len(parts),
            bytes_accessed=2 * inner * sub * len(parts),
            transcendentals=0,
        ),
    )(hidden, weight)


def add_kernel(own_ref, x_ref, hidden_ref, out, hidden_out):
    out[...] = (own_ref[...].astype(f32) + x_ref[...].astype(f32)).astype(bf16)


def add_step(own, x, hidden):
    vmem = pl.BlockSpec(memory_space=pltpu.VMEM)
    return pl.pallas_call(
        add_kernel,
        out_shape=[pltpu.VMEM(x.shape, bf16), pltpu.VMEM(hidden.shape, bf16)],
        in_specs=[vmem] * 3,
        out_specs=[vmem] * 2,
        input_output_aliases={2: 1},
        compiler_params=pltpu.CompilerParams(vmem_limit_bytes=12 * MIB),
        cost_estimate=pl.CostEstimate(flops=x.size, bytes_accessed=6 * x.size, transcendentals=0),
    )(own, x, hidden)


def finish_kernel(half, own_ref, residual_ref, x_ref, y_ref, out):
    sub = out.shape[1]
    total = own_ref[...].astype(f32) + residual_ref[:, half * sub : (half + 1) * sub].astype(f32)
    out[...] = (total + x_ref[...].astype(f32) + y_ref[...].astype(f32)).astype(bf16)


def finish(half, own, residual, x, y):
    vmem = pl.BlockSpec(memory_space=pltpu.VMEM)
    return pl.pallas_call(
        functools.partial(finish_kernel, half),
        out_shape=[pltpu.VMEM(own.shape, bf16)],
        in_specs=[vmem] * 4,
        out_specs=[vmem],
        compiler_params=pltpu.CompilerParams(vmem_limit_bytes=12 * MIB),
        cost_estimate=pl.CostEstimate(flops=4 * own.size, bytes_accessed=10 * own.size, transcendentals=0),
    )(own, residual, x, y)[0]


def qkv_kernel(n, parts, first, last, joins, total_features, *refs):
    count = len(parts)
    xs, (gain_ref, w_ref), rest = refs[:count], refs[count : count + 2], refs[count + 2 :]
    sub = xs[0].shape[-1]
    if not first:
        total_in, squares_in, rest = rest[0], rest[1], rest[2:]
    if joins:
        for i, x_ref in enumerate(xs[-2:]):
            rest[2][:, i * sub : (i + 1) * sub] = x_ref[...]
    columns = w_ref.shape[1]
    scaled, rows_at = [], []
    squares = None if first else squares_in[...]
    for x_ref, (offset, half) in zip(xs, parts):
        row = pl.multiple_of(owner(n, offset) * (2 * sub) + half * sub, sub)
        x = x_ref[...].astype(f32)
        scaled.append((x * gain_ref[:, pl.ds(row, sub)]).astype(bf16))
        rows_at.append(row)
        for c in range(0, sub, 128):
            piece = x[:, c : c + 128]
            squares = piece * piece if squares is None else squares + piece * piece
    if last:
        mean = jnp.sum(squares, axis=1, keepdims=True) / total_features
        scale = jnp.sqrt(mean + epsilon)
        inverse = 1.0 / scale
    else:
        rest[1][...] = squares
    for c in range(0, columns, 256):
        wide = min(256, columns - c)
        acc = None if first else total_in[:, c : c + wide]
        for x, row in zip(scaled, rows_at):
            more = jnp.dot(x, w_ref[pl.ds(row, sub), c : c + wide], preferred_element_type=f32)
            acc = more if acc is None else acc + more
        if last:
            rest[0][:, c : c + wide] = (acc * inverse).astype(bf16)
        else:
            rest[0][:, c : c + wide] = acc


def qkv_step(n, parts, xs, gain, weight, state, last=False, hand_on=False, joins=False):
    rows, sub = xs[0].shape
    columns = weight.shape[1]
    vmem = pl.BlockSpec(memory_space=pltpu.VMEM)
    if last:
        out_shape = [jax.ShapeDtypeStruct((rows, columns), bf16)]
    else:
        out_shape = [pltpu.VMEM((rows, columns), f32), pltpu.VMEM((rows, 128), f32)]
    aliases = {}
    if joins:
        out_shape.append(jax.ShapeDtypeStruct((rows, 2 * sub), bf16))
    if hand_on:
        aliases = {len(xs) - 1: len(out_shape)}
        out_shape.append(pltpu.VMEM((rows, sub), bf16))
    operands = (*xs, gain, weight, *state)
    return pl.pallas_call(
        functools.partial(qkv_kernel, n, parts, not state, last, joins, float(weight.shape[0])),
        out_shape=out_shape,
        in_specs=[vmem] * len(operands),
        out_specs=[vmem] * len(out_shape),
        input_output_aliases=aliases,
        compiler_params=pltpu.CompilerParams(vmem_limit_bytes=16 * MIB),
        cost_estimate=pl.CostEstimate(
            flops=2 * rows * sub * columns * len(parts),
            bytes_accessed=2 * sub * columns * len(parts),
            transcendentals=0,
        ),
    )(*operands)


def make_shards(n):
    order = ring_order(n)
    right = [(order[p], order[(p + 1) % n]) for p in range(n)]
    left = [(order[p], order[(p - 1) % n]) for p in range(n)]
    half = n // 2
    plan = [((half, 0), (half, 1))]
    for k in range(half - 1, 0, -1):
        plan += [((k, 1), (-k, 0)), ((k, 0), (-k, 1))]

    def shards(hidden, down_weight, residual, norm_gain, qkv_weight):
        rows, width = residual.shape
        sub = width // 2

        def send(x, pairs):
            return lax.ppermute(x, "tensor", pairs)

        *own, hidden = down(n, plan[0], hidden, down_weight, sub, first=True)
        arrived = [(send(own[0], right), send(own[1], left))]
        for step in range(1, n - 1, 2):
            own = down(n, [*plan[step], *plan[step + 1]], hidden, down_weight, sub)
            for i in range(2):
                up, down_ = own[2 * i : 2 * i + 2]
                if step + i > 1:
                    from_left, from_right = arrived[-2]
                    down_, hidden = add_step(down_, from_right, hidden)
                    up, hidden = add_step(up, from_left, hidden)
                arrived.append((send(up, right), send(down_, left)))
        own = down(n, [(0, 0), (0, 1)], hidden, down_weight, sub)
        (left_b, right_a), (left_a, right_b) = arrived[-2:]
        halves = [finish(0, own[0], residual, left_a, right_a), finish(1, own[1], residual, left_b, right_b)]

        gain = norm_gain[None, :]
        arrived = [(send(halves[0], right), send(halves[1], left))]
        arrived.append((send(halves[1], right), send(halves[0], left)))
        state, parts, xs = (), [], []
        for step in range(n - 1):
            x, y = arrived[step]
            k = step // 2 + 1
            parts += [(k, 1 - step % 2), (-k, step % 2)]
            xs += [y, x]
            if step in (n - 4, n - 5):
                arrived.append((send(x, right), send(y, left)))
            elif step == n - 3:
                state = qkv_step(n, parts, xs, gain, qkv_weight, state)
                *state, stream = qkv_step(n, [(0, 0), (0, 1)], halves, gain, qkv_weight, state, joins=True)
                parts, xs = [], []
            elif step == n - 2:
                state = qkv_step(n, parts[:1], xs[:1], gain, qkv_weight, state)
                (qkv,) = qkv_step(n, parts[1:], xs[1:], gain, qkv_weight, state, last=True)
            else:
                *state, x = qkv_step(n, parts, xs, gain, qkv_weight, state, hand_on=True)
                arrived.append((send(x, right), send(y, left)))
                parts, xs = [], []
        return stream, qkv

    return shards


def solution(mesh):
    in_specs = (P("dp", "tensor"), P("tensor", None), P("dp", "tensor"), P(), P(None, "tensor"))
    out_specs = (P("dp", "tensor"), P("dp", "tensor"))
    return jax.shard_map(
        make_shards(mesh.shape["tensor"]),
        mesh=mesh,
        in_specs=in_specs,
        out_specs=out_specs,
        check_vma=False,
    )
```

```python
import functools

import jax
import jax.numpy as jnp
from jax import lax
from jax.experimental import pallas as pl
from jax.experimental.pallas import tpu as pltpu
from jax.sharding import PartitionSpec as P

epsilon = 1e-05
f32, bf16 = jnp.float32, jnp.bfloat16
MIB = 1024 * 1024


def ring_order(n):
    return list(range(0, n, 2)) + list(range(n - 1, 0, -2))


def owner(n, offset):
    me = lax.axis_index("tensor")
    place = jnp.where(me % 2 == 0, me // 2, n - 1 - me // 2)
    place = (place + (offset + n)) % n
    return jnp.where(place < n // 2, 2 * place, 2 * (n - 1 - place) + 1)


def down_kernel(n, parts, x_ref, w_ref, *rest):
    outs, rest = rest[: len(parts)], list(rest[len(parts) :])
    buf, sems = rest[-2:]
    if len(rest) > 2:
        x_out, x_sem = rest[:2]
        x_copy = pltpu.make_async_copy(x_ref, x_out, x_sem)
        x_copy.start()
    else:
        x_out, x_copy = x_ref, None
    sub = outs[0].shape[1]
    per, (count, pieces) = sub // buf.shape[2], sems.shape
    tile, deep = buf.shape[2], buf.shape[1] // pieces

    def copies(i, begin, j):
        at = i * per + j
        columns = pl.ds(pl.multiple_of(begin + j * tile, tile), tile)
        for p in range(pieces):
            rows = pl.ds(p * deep, deep)
            yield pltpu.make_async_copy(w_ref.at[rows, columns], buf.at[at, rows], sems.at[at, p])

    begins = [owner(n, offset) * (2 * sub) + half * sub for offset, half in parts]
    for i in range(len(parts)):
        for j in range(per):
            for copy in copies(i, begins[i], j):
                copy.start()
    if x_copy is not None:
        x_copy.wait()
    for i, out in enumerate(outs):

        def step(j, carry):
            for copy in copies(i, begins[i], j):
                copy.wait()
            part = jnp.dot(x_out[...], buf[i * per + j], preferred_element_type=f32)
            out[:, pl.ds(pl.multiple_of(j * tile, tile), tile)] = part.astype(bf16)
            return carry

        lax.fori_loop(0, per, step, 0)


def down(n, parts, hidden, down_weight, sub, first=False):
    rows, inner = hidden.shape
    vmem, hbm = pl.BlockSpec(memory_space=pltpu.VMEM), pl.BlockSpec(memory_space=pltpu.HBM)
    pieces = max(p for p in (1, 2) if inner % (16 * p) == 0)
    tile = sub
    count = len(parts) * (sub // tile)
    weight = pltpu.with_memory_space_constraint(down_weight, pltpu.HBM)
    out_shape = [pltpu.VMEM((rows, sub), bf16)] * len(parts)
    scratch = [pltpu.VMEM((count, inner, tile), bf16), pltpu.SemaphoreType.DMA((count, pieces))]
    if first:
        hidden = pltpu.with_memory_space_constraint(hidden, pltpu.HBM)
        out_shape = out_shape + [pltpu.VMEM(hidden.shape, bf16)]
        scratch = [pltpu.SemaphoreType.DMA] + scratch
    return pl.pallas_call(
        functools.partial(down_kernel, n, parts),
        out_shape=out_shape,
        in_specs=[hbm if first else vmem, hbm],
        out_specs=[vmem] * len(out_shape),
        scratch_shapes=scratch,
        compiler_params=pltpu.CompilerParams(vmem_limit_bytes=14 * MIB),
        cost_estimate=pl.CostEstimate(
            flops=2 * rows * inner * sub * len(parts),
            bytes_accessed=2 * inner * sub * len(parts),
            transcendentals=0,
        ),
    )(hidden, weight)


def add_kernel(own_ref, x_ref, hidden_ref, out, hidden_out):
    out[...] = (own_ref[...].astype(f32) + x_ref[...].astype(f32)).astype(bf16)


def add_step(own, x, hidden):
    vmem = pl.BlockSpec(memory_space=pltpu.VMEM)
    return pl.pallas_call(
        add_kernel,
        out_shape=[pltpu.VMEM(x.shape, bf16), pltpu.VMEM(hidden.shape, bf16)],
        in_specs=[vmem] * 3,
        out_specs=[vmem] * 2,
        input_output_aliases={2: 1},
        compiler_params=pltpu.CompilerParams(vmem_limit_bytes=12 * MIB),
        cost_estimate=pl.CostEstimate(flops=x.size, bytes_accessed=6 * x.size, transcendentals=0),
    )(own, x, hidden)


def finish_kernel(half, own_ref, residual_ref, x_ref, y_ref, out):
    sub = out.shape[1]
    total = own_ref[...].astype(f32) + residual_ref[:, half * sub : (half + 1) * sub].astype(f32)
    out[...] = (total + x_ref[...].astype(f32) + y_ref[...].astype(f32)).astype(bf16)


def finish(half, own, residual, x, y):
    vmem = pl.BlockSpec(memory_space=pltpu.VMEM)
    return pl.pallas_call(
        functools.partial(finish_kernel, half),
        out_shape=[pltpu.VMEM(own.shape, bf16)],
        in_specs=[vmem] * 4,
        out_specs=[vmem],
        compiler_params=pltpu.CompilerParams(vmem_limit_bytes=12 * MIB),
        cost_estimate=pl.CostEstimate(flops=4 * own.size, bytes_accessed=10 * own.size, transcendentals=0),
    )(own, residual, x, y)[0]


def qkv_kernel(n, parts, first, last, joins, total_features, *refs):
    count = len(parts)
    xs, (gain_ref, w_ref), rest = refs[:count], refs[count : count + 2], refs[count + 2 :]
    sub = xs[0].shape[-1]
    if not first:
        total_in, squares_in, rest = rest[0], rest[1], rest[2:]
    if joins:
        for i, x_ref in enumerate(xs[-2:]):
            rest[2][:, i * sub : (i + 1) * sub] = x_ref[...]
    columns = w_ref.shape[1]
    scaled, rows_at = [], []
    squares = None if first else squares_in[...]
    for x_ref, (offset, half) in zip(xs, parts):
        row = pl.multiple_of(owner(n, offset) * (2 * sub) + half * sub, sub)
        x = x_ref[...].astype(f32)
        scaled.append((x * gain_ref[:, pl.ds(row, sub)]).astype(bf16))
        rows_at.append(row)
        for c in range(0, sub, 128):
            piece = x[:, c : c + 128]
            squares = piece * piece if squares is None else squares + piece * piece
    if last:
        mean = jnp.sum(squares, axis=1, keepdims=True) / total_features
        scale = jnp.sqrt(mean + epsilon)
        inverse = 1.0 / scale
    else:
        rest[1][...] = squares
    for c in range(0, columns, 256):
        wide = min(256, columns - c)
        acc = None if first else total_in[:, c : c + wide]
        for x, row in zip(scaled, rows_at):
            more = jnp.dot(x, w_ref[pl.ds(row, sub), c : c + wide], preferred_element_type=f32)
            acc = more if acc is None else acc + more
        if last:
            rest[0][:, c : c + wide] = (acc * inverse).astype(bf16)
        else:
            rest[0][:, c : c + wide] = acc


def qkv_step(n, parts, xs, gain, weight, state, last=False, hand_on=False, joins=False):
    rows, sub = xs[0].shape
    columns = weight.shape[1]
    vmem = pl.BlockSpec(memory_space=pltpu.VMEM)
    if last:
        out_shape = [jax.ShapeDtypeStruct((rows, columns), bf16)]
    else:
        out_shape = [pltpu.VMEM((rows, columns), f32), pltpu.VMEM((rows, 128), f32)]
    aliases = {}
    if joins:
        out_shape.append(jax.ShapeDtypeStruct((rows, 2 * sub), bf16))
    if hand_on:
        aliases = {len(xs) - 1: len(out_shape)}
        out_shape.append(pltpu.VMEM((rows, sub), bf16))
    operands = (*xs, gain, weight, *state)
    return pl.pallas_call(
        functools.partial(qkv_kernel, n, parts, not state, last, joins, float(weight.shape[0])),
        out_shape=out_shape,
        in_specs=[vmem] * len(operands),
        out_specs=[vmem] * len(out_shape),
        input_output_aliases=aliases,
        compiler_params=pltpu.CompilerParams(vmem_limit_bytes=16 * MIB),
        cost_estimate=pl.CostEstimate(
            flops=2 * rows * sub * columns * len(parts),
            bytes_accessed=2 * sub * columns * len(parts),
            transcendentals=0,
        ),
    )(*operands)


def make_shards(n):
    order = ring_order(n)
    right = [(order[p], order[(p + 1) % n]) for p in range(n)]
    left = [(order[p], order[(p - 1) % n]) for p in range(n)]
    half = n // 2
    plan = [((half, 0), (half, 1))]
    for k in range(half - 1, 0, -1):
        plan += [((k, 1), (-k, 0)), ((k, 0), (-k, 1))]

    def shards(hidden, down_weight, residual, norm_gain, qkv_weight):
        rows, width = residual.shape
        sub = width // 2

        def send(x, pairs):
            return lax.ppermute(x, "tensor", pairs)

        *own, hidden = down(n, plan[0], hidden, down_weight, sub, first=True)
        arrived = [(send(own[0], right), send(own[1], left))]
        for step in range(1, n - 1, 2):
            own = down(n, [*plan[step], *plan[step + 1]], hidden, down_weight, sub)
            for i in range(2):
                up, down_ = own[2 * i : 2 * i + 2]
                if step + i > 1:
                    from_left, from_right = arrived[-2]
                    down_, hidden = add_step(down_, from_right, hidden)
                    up, hidden = add_step(up, from_left, hidden)
                arrived.append((send(up, right), send(down_, left)))
        own = down(n, [(0, 0), (0, 1)], hidden, down_weight, sub)
        (left_b, right_a), (left_a, right_b) = arrived[-2:]
        halves = [finish(0, own[0], residual, left_a, right_a), finish(1, own[1], residual, left_b, right_b)]

        gain = norm_gain[None, :]
        arrived = [(send(halves[0], right), send(halves[1], left))]
        arrived.append((send(halves[1], right), send(halves[0], left)))
        state, parts, xs = (), [], []
        for step in range(n - 1):
            x, y = arrived[step]
            k = step // 2 + 1
            parts += [(k, 1 - step % 2), (-k, step % 2)]
            xs += [y, x]
            if step in (n - 4, n - 5):
                arrived.append((send(x, right), send(y, left)))
            elif step == n - 3:
                state = qkv_step(n, parts, xs, gain, qkv_weight, state)
                *state, stream = qkv_step(n, [(0, 0), (0, 1)], halves, gain, qkv_weight, state, joins=True)
                parts, xs = [], []
            elif step == n - 2:
                state = qkv_step(n, parts[:1], xs[:1], gain, qkv_weight, state)
                (qkv,) = qkv_step(n, parts[1:], xs[1:], gain, qkv_weight, state, last=True)
            else:
                *state, x = qkv_step(n, parts, xs, gain, qkv_weight, state, hand_on=True)
                arrived.append((send(x, right), send(y, left)))
                parts, xs = [], []
        return stream, qkv

    return shards


def solution(mesh):
    in_specs = (P("dp", "tensor"), P("tensor", None), P("dp", "tensor"), P(), P(None, "tensor"))
    out_specs = (P("dp", "tensor"), P("dp", "tensor"))
    return jax.shard_map(
        make_shards(mesh.shape["tensor"]),
        mesh=mesh,
        in_specs=in_specs,
        out_specs=out_specs,
        check_vma=False,
    )
```

```python
import functools

import jax
import jax.numpy as jnp
from jax import lax
from jax.experimental import pallas as pl
from jax.experimental.pallas import tpu as pltpu
from jax.sharding import PartitionSpec as P

epsilon = 1e-05
f32, bf16 = jnp.float32, jnp.bfloat16
MIB = 1024 * 1024


def ring_order(n):
    return list(range(0, n, 2)) + list(range(n - 1, 0, -2))


def owner(n, offset):
    me = lax.axis_index("tensor")
    place = jnp.where(me % 2 == 0, me // 2, n - 1 - me // 2)
    place = (place + (offset + n)) % n
    return jnp.where(place < n // 2, 2 * place, 2 * (n - 1 - place) + 1)


def down_kernel(n, parts, x_ref, w_ref, *rest):
    outs, rest = rest[: len(parts)], list(rest[len(parts) :])
    buf, sems = rest[-2:]
    if len(rest) > 2:
        x_out, x_sem = rest[:2]
        x_copy = pltpu.make_async_copy(x_ref, x_out, x_sem)
        x_copy.start()
    else:
        x_out, x_copy = x_ref, None
    sub = outs[0].shape[1]
    per, (count, pieces) = sub // buf.shape[2], sems.shape
    tile, deep = buf.shape[2], buf.shape[1] // pieces

    def copies(i, begin, j):
        at = i * per + j
        columns = pl.ds(pl.multiple_of(begin + j * tile, tile), tile)
        for p in range(pieces):
            rows = pl.ds(p * deep, deep)
            yield pltpu.make_async_copy(w_ref.at[rows, columns], buf.at[at, rows], sems.at[at, p])

    begins = [owner(n, offset) * (2 * sub) + half * sub for offset, half in parts]
    for i in range(len(parts)):
        for j in range(per):
            for copy in copies(i, begins[i], j):
                copy.start()
    if x_copy is not None:
        x_copy.wait()
    for i, out in enumerate(outs):

        def step(j, carry):
            for copy in copies(i, begins[i], j):
                copy.wait()
            part = jnp.dot(x_out[...], buf[i * per + j], preferred_element_type=f32)
            out[:, pl.ds(pl.multiple_of(j * tile, tile), tile)] = part.astype(bf16)
            return carry

        lax.fori_loop(0, per, step, 0)


def down(n, parts, hidden, down_weight, sub, first=False):
    rows, inner = hidden.shape
    vmem, hbm = pl.BlockSpec(memory_space=pltpu.VMEM), pl.BlockSpec(memory_space=pltpu.HBM)
    pieces = max(p for p in (1, 2) if inner % (16 * p) == 0)
    tile = sub
    count = len(parts) * (sub // tile)
    weight = pltpu.with_memory_space_constraint(down_weight, pltpu.HBM)
    out_shape = [pltpu.VMEM((rows, sub), bf16)] * len(parts)
    scratch = [pltpu.VMEM((count, inner, tile), bf16), pltpu.SemaphoreType.DMA((count, pieces))]
    if first:
        hidden = pltpu.with_memory_space_constraint(hidden, pltpu.HBM)
        out_shape = out_shape + [pltpu.VMEM(hidden.shape, bf16)]
        scratch = [pltpu.SemaphoreType.DMA] + scratch
    return pl.pallas_call(
        functools.partial(down_kernel, n, parts),
        out_shape=out_shape,
        in_specs=[hbm if first else vmem, hbm],
        out_specs=[vmem] * len(out_shape),
        scratch_shapes=scratch,
        compiler_params=pltpu.CompilerParams(vmem_limit_bytes=14 * MIB),
        cost_estimate=pl.CostEstimate(
            flops=2 * rows * inner * sub * len(parts),
            bytes_accessed=2 * inner * sub * len(parts),
            transcendentals=0,
        ),
    )(hidden, weight)


def add_kernel(own_ref, x_ref, hidden_ref, out, hidden_out):
    out[...] = (own_ref[...].astype(f32) + x_ref[...].astype(f32)).astype(bf16)


def add_step(own, x, hidden):
    vmem = pl.BlockSpec(memory_space=pltpu.VMEM)
    return pl.pallas_call(
        add_kernel,
        out_shape=[pltpu.VMEM(x.shape, bf16), pltpu.VMEM(hidden.shape, bf16)],
        in_specs=[vmem] * 3,
        out_specs=[vmem] * 2,
        input_output_aliases={2: 1},
        compiler_params=pltpu.CompilerParams(vmem_limit_bytes=12 * MIB),
        cost_estimate=pl.CostEstimate(flops=x.size, bytes_accessed=6 * x.size, transcendentals=0),
    )(own, x, hidden)


def finish_kernel(half, own_ref, residual_ref, x_ref, y_ref, out):
    sub = out.shape[1]
    total = own_ref[...].astype(f32) + residual_ref[:, half * sub : (half + 1) * sub].astype(f32)
    out[...] = (total + x_ref[...].astype(f32) + y_ref[...].astype(f32)).astype(bf16)


def finish(half, own, residual, x, y):
    vmem = pl.BlockSpec(memory_space=pltpu.VMEM)
    return pl.pallas_call(
        functools.partial(finish_kernel, half),
        out_shape=[pltpu.VMEM(own.shape, bf16)],
        in_specs=[vmem] * 4,
        out_specs=[vmem],
        compiler_params=pltpu.CompilerParams(vmem_limit_bytes=12 * MIB),
        cost_estimate=pl.CostEstimate(flops=4 * own.size, bytes_accessed=10 * own.size, transcendentals=0),
    )(own, residual, x, y)[0]


def qkv_kernel(n, parts, first, last, joins, total_features, *refs):
    count = len(parts)
    xs, (gain_ref, w_ref), rest = refs[:count], refs[count : count + 2], refs[count + 2 :]
    sub = xs[0].shape[-1]
    if not first:
        total_in, squares_in, rest = rest[0], rest[1], rest[2:]
    if joins:
        for i, x_ref in enumerate(xs[-2:]):
            rest[2][:, i * sub : (i + 1) * sub] = x_ref[...]
    columns = w_ref.shape[1]
    scaled, rows_at = [], []
    squares = None if first else squares_in[...]
    for x_ref, (offset, half) in zip(xs, parts):
        row = pl.multiple_of(owner(n, offset) * (2 * sub) + half * sub, sub)
        x = x_ref[...].astype(f32)
        scaled.append((x * gain_ref[:, pl.ds(row, sub)]).astype(bf16))
        rows_at.append(row)
        for c in range(0, sub, 128):
            piece = x[:, c : c + 128]
            squares = piece * piece if squares is None else squares + piece * piece
    if last:
        mean = jnp.sum(squares, axis=1, keepdims=True) / total_features
        scale = jnp.sqrt(mean + epsilon)
        inverse = 1.0 / scale
    else:
        rest[1][...] = squares
    for c in range(0, columns, 256):
        wide = min(256, columns - c)
        acc = None if first else total_in[:, c : c + wide]
        for x, row in zip(scaled, rows_at):
            more = jnp.dot(x, w_ref[pl.ds(row, sub), c : c + wide], preferred_element_type=f32)
            acc = more if acc is None else acc + more
        if last:
            rest[0][:, c : c + wide] = (acc * inverse).astype(bf16)
        else:
            rest[0][:, c : c + wide] = acc


def qkv_step(n, parts, xs, gain, weight, state, last=False, hand_on=False, joins=False):
    rows, sub = xs[0].shape
    columns = weight.shape[1]
    vmem = pl.BlockSpec(memory_space=pltpu.VMEM)
    if last:
        out_shape = [jax.ShapeDtypeStruct((rows, columns), bf16)]
    else:
        out_shape = [pltpu.VMEM((rows, columns), f32), pltpu.VMEM((rows, 128), f32)]
    aliases = {}
    if joins:
        out_shape.append(jax.ShapeDtypeStruct((rows, 2 * sub), bf16))
    if hand_on:
        aliases = {len(xs) - 1: len(out_shape)}
        out_shape.append(pltpu.VMEM((rows, sub), bf16))
    operands = (*xs, gain, weight, *state)
    return pl.pallas_call(
        functools.partial(qkv_kernel, n, parts, not state, last, joins, float(weight.shape[0])),
        out_shape=out_shape,
        in_specs=[vmem] * len(operands),
        out_specs=[vmem] * len(out_shape),
        input_output_aliases=aliases,
        compiler_params=pltpu.CompilerParams(vmem_limit_bytes=16 * MIB),
        cost_estimate=pl.CostEstimate(
            flops=2 * rows * sub * columns * len(parts),
            bytes_accessed=2 * sub * columns * len(parts),
            transcendentals=0,
        ),
    )(*operands)


def make_shards(n):
    order = ring_order(n)
    right = [(order[p], order[(p + 1) % n]) for p in range(n)]
    left = [(order[p], order[(p - 1) % n]) for p in range(n)]
    half = n // 2
    plan = [((half, 0), (half, 1))]
    for k in range(half - 1, 0, -1):
        plan += [((k, 1), (-k, 0)), ((k, 0), (-k, 1))]

    def shards(hidden, down_weight, residual, norm_gain, qkv_weight):
        rows, width = residual.shape
        sub = width // 2

        def send(x, pairs):
            return lax.ppermute(x, "tensor", pairs)

        *own, hidden = down(n, plan[0], hidden, down_weight, sub, first=True)
        arrived = [(send(own[0], right), send(own[1], left))]
        for group in [plan[1:2], plan[2:3]] + [plan[s : s + 2] for s in range(3, n - 1, 2)]:
            own = down(n, [part for pair in group for part in pair], hidden, down_weight, sub)
            for i in range(0, len(own), 2):
                up, down_ = own[i : i + 2]
                if len(arrived) > 1:
                    from_left, from_right = arrived[-2]
                    down_, hidden = add_step(down_, from_right, hidden)
                    up, hidden = add_step(up, from_left, hidden)
                arrived.append((send(up, right), send(down_, left)))
        own = down(n, [(0, 0), (0, 1)], hidden, down_weight, sub)
        (left_b, right_a), (left_a, right_b) = arrived[-2:]
        halves = [finish(0, own[0], residual, left_a, right_a), finish(1, own[1], residual, left_b, right_b)]

        gain = norm_gain[None, :]
        arrived = [(send(halves[0], right), send(halves[1], left))]
        arrived.append((send(halves[1], right), send(halves[0], left)))
        state, parts, xs = (), [], []
        for step in range(n - 1):
            x, y = arrived[step]
            k = step // 2 + 1
            parts += [(k, 1 - step % 2), (-k, step % 2)]
            xs += [y, x]
            if step in (n - 4, n - 5):
                arrived.append((send(x, right), send(y, left)))
            elif step == n - 3:
                state = qkv_step(n, parts, xs, gain, qkv_weight, state)
                *state, stream = qkv_step(n, [(0, 0), (0, 1)], halves, gain, qkv_weight, state, joins=True)
                parts, xs = [], []
            elif step == n - 2:
                state = qkv_step(n, parts[:1], xs[:1], gain, qkv_weight, state)
                (qkv,) = qkv_step(n, parts[1:], xs[1:], gain, qkv_weight, state, last=True)
            else:
                *state, x = qkv_step(n, parts, xs, gain, qkv_weight, state, hand_on=True)
                arrived.append((send(x, right), send(y, left)))
                parts, xs = [], []
        return stream, qkv

    return shards


def solution(mesh):
    in_specs = (P("dp", "tensor"), P("tensor", None), P("dp", "tensor"), P(), P(None, "tensor"))
    out_specs = (P("dp", "tensor"), P("dp", "tensor"))
    return jax.shard_map(
        make_shards(mesh.shape["tensor"]),
        mesh=mesh,
        in_specs=in_specs,
        out_specs=out_specs,
        check_vma=False,
    )
```

```python
import functools

import jax
import jax.numpy as jnp
from jax import lax
from jax.experimental import pallas as pl
from jax.experimental.pallas import tpu as pltpu
from jax.sharding import PartitionSpec as P

epsilon = 1e-05
f32, bf16 = jnp.float32, jnp.bfloat16
MIB = 1024 * 1024


def ring_order(n):
    return list(range(0, n, 2)) + list(range(n - 1, 0, -2))


def owner(n, offset):
    me = lax.axis_index("tensor")
    place = jnp.where(me % 2 == 0, me // 2, n - 1 - me // 2)
    place = (place + (offset + n)) % n
    return jnp.where(place < n // 2, 2 * place, 2 * (n - 1 - place) + 1)


def down_kernel(n, parts, x_ref, w_ref, *rest):
    outs, rest = rest[: len(parts)], list(rest[len(parts) :])
    buf, sems = rest[-2:]
    if len(rest) > 2:
        x_out, x_sem = rest[:2]
        x_copy = pltpu.make_async_copy(x_ref, x_out, x_sem)
        x_copy.start()
    else:
        x_out, x_copy = x_ref, None
    sub = outs[0].shape[1]
    per, (count, pieces) = sub // buf.shape[2], sems.shape
    tile, deep = buf.shape[2], buf.shape[1] // pieces

    def copies(i, begin, j):
        at = i * per + j
        columns = pl.ds(pl.multiple_of(begin + j * tile, tile), tile)
        for p in range(pieces):
            rows = pl.ds(p * deep, deep)
            yield pltpu.make_async_copy(w_ref.at[rows, columns], buf.at[at, rows], sems.at[at, p])

    begins = [owner(n, offset) * (2 * sub) + half * sub for offset, half in parts]
    for i in range(len(parts)):
        for j in range(per):
            for copy in copies(i, begins[i], j):
                copy.start()
    if x_copy is not None:
        x_copy.wait()
    for i, out in enumerate(outs):

        def step(j, carry):
            for copy in copies(i, begins[i], j):
                copy.wait()
            part = jnp.dot(x_out[...], buf[i * per + j], preferred_element_type=f32)
            out[:, pl.ds(pl.multiple_of(j * tile, tile), tile)] = part.astype(bf16)
            return carry

        lax.fori_loop(0, per, step, 0)


def down(n, parts, hidden, down_weight, sub, first=False):
    rows, inner = hidden.shape
    vmem, hbm = pl.BlockSpec(memory_space=pltpu.VMEM), pl.BlockSpec(memory_space=pltpu.HBM)
    pieces = max(p for p in (1, 2) if inner % (16 * p) == 0)
    tile = sub
    count = len(parts) * (sub // tile)
    weight = pltpu.with_memory_space_constraint(down_weight, pltpu.HBM)
    out_shape = [pltpu.VMEM((rows, sub), bf16)] * len(parts)
    scratch = [pltpu.VMEM((count, inner, tile), bf16), pltpu.SemaphoreType.DMA((count, pieces))]
    if first:
        hidden = pltpu.with_memory_space_constraint(hidden, pltpu.HBM)
        out_shape = out_shape + [pltpu.VMEM(hidden.shape, bf16)]
        scratch = [pltpu.SemaphoreType.DMA] + scratch
    return pl.pallas_call(
        functools.partial(down_kernel, n, parts),
        out_shape=out_shape,
        in_specs=[hbm if first else vmem, hbm],
        out_specs=[vmem] * len(out_shape),
        scratch_shapes=scratch,
        compiler_params=pltpu.CompilerParams(vmem_limit_bytes=14 * MIB),
        cost_estimate=pl.CostEstimate(
            flops=2 * rows * inner * sub * len(parts),
            bytes_accessed=2 * inner * sub * len(parts),
            transcendentals=0,
        ),
    )(hidden, weight)


def add_kernel(own_ref, x_ref, hidden_ref, out, hidden_out):
    out[...] = (own_ref[...].astype(f32) + x_ref[...].astype(f32)).astype(bf16)


def add_step(own, x, hidden):
    vmem = pl.BlockSpec(memory_space=pltpu.VMEM)
    return pl.pallas_call(
        add_kernel,
        out_shape=[pltpu.VMEM(x.shape, bf16), pltpu.VMEM(hidden.shape, bf16)],
        in_specs=[vmem] * 3,
        out_specs=[vmem] * 2,
        input_output_aliases={2: 1},
        compiler_params=pltpu.CompilerParams(vmem_limit_bytes=12 * MIB),
        cost_estimate=pl.CostEstimate(flops=x.size, bytes_accessed=6 * x.size, transcendentals=0),
    )(own, x, hidden)


def finish_kernel(half, own_ref, residual_ref, x_ref, y_ref, out):
    sub = out.shape[1]
    total = own_ref[...].astype(f32) + residual_ref[:, half * sub : (half + 1) * sub].astype(f32)
    out[...] = (total + x_ref[...].astype(f32) + y_ref[...].astype(f32)).astype(bf16)


def finish(half, own, residual, x, y):
    vmem = pl.BlockSpec(memory_space=pltpu.VMEM)
    return pl.pallas_call(
        functools.partial(finish_kernel, half),
        out_shape=[pltpu.VMEM(own.shape, bf16)],
        in_specs=[vmem] * 4,
        out_specs=[vmem],
        compiler_params=pltpu.CompilerParams(vmem_limit_bytes=12 * MIB),
        cost_estimate=pl.CostEstimate(flops=4 * own.size, bytes_accessed=10 * own.size, transcendentals=0),
    )(own, residual, x, y)[0]


def qkv_kernel(n, parts, first, last, joins, total_features, *refs):
    count = len(parts)
    xs, (gain_ref, w_ref), rest = refs[:count], refs[count : count + 2], refs[count + 2 :]
    sub = xs[0].shape[-1]
    if not first:
        total_in, squares_in, rest = rest[0], rest[1], rest[2:]
    if joins:
        for i, x_ref in enumerate(xs[-2:]):
            rest[2][:, i * sub : (i + 1) * sub] = x_ref[...]
    columns = w_ref.shape[1]
    scaled, rows_at = [], []
    squares = None if first else squares_in[...]
    for x_ref, (offset, half) in zip(xs, parts):
        row = pl.multiple_of(owner(n, offset) * (2 * sub) + half * sub, sub)
        x = x_ref[...].astype(f32)
        scaled.append((x * gain_ref[:, pl.ds(row, sub)]).astype(bf16))
        rows_at.append(row)
        for c in range(0, sub, 128):
            piece = x[:, c : c + 128]
            squares = piece * piece if squares is None else squares + piece * piece
    if last:
        mean = jnp.sum(squares, axis=1, keepdims=True) / total_features
        scale = jnp.sqrt(mean + epsilon)
        inverse = 1.0 / scale
    else:
        rest[1][...] = squares
    copies = []
    for c in range(0, columns, 256):
        wide = min(256, columns - c)
        acc = None if first else total_in[:, c : c + wide]
        for x, row in zip(scaled, rows_at):
            more = jnp.dot(x, w_ref[pl.ds(row, sub), c : c + wide], preferred_element_type=f32)
            acc = more if acc is None else acc + more
        if last:
            out, ready, sems = rest
            ready[:, c : c + wide] = (acc * inverse).astype(bf16)
            tile = ready.at[:, pl.ds(c, wide)]
            copies.append(pltpu.make_async_copy(tile, out.at[:, pl.ds(c, wide)], sems.at[len(copies)]))
            copies[-1].start()
        else:
            rest[0][:, c : c + wide] = acc
    for copy in copies:
        copy.wait()


def qkv_step(n, parts, xs, gain, weight, state, last=False, hand_on=False, joins=False):
    rows, sub = xs[0].shape
    columns = weight.shape[1]
    vmem = pl.BlockSpec(memory_space=pltpu.VMEM)
    scratch = []
    if last:
        out_shape = [jax.ShapeDtypeStruct((rows, columns), bf16)]
        scratch = [pltpu.VMEM((rows, columns), bf16), pltpu.SemaphoreType.DMA((pl.cdiv(columns, 256),))]
    else:
        out_shape = [pltpu.VMEM((rows, columns), f32), pltpu.VMEM((rows, 128), f32)]
    aliases = {}
    if joins:
        out_shape.append(jax.ShapeDtypeStruct((rows, 2 * sub), bf16))
    if hand_on:
        aliases = {len(xs) - 1: len(out_shape)}
        out_shape.append(pltpu.VMEM((rows, sub), bf16))
    operands = (*xs, gain, weight, *state)
    return pl.pallas_call(
        functools.partial(qkv_kernel, n, parts, not state, last, joins, float(weight.shape[0])),
        out_shape=out_shape,
        in_specs=[vmem] * len(operands),
        out_specs=[pl.BlockSpec(memory_space=pltpu.HBM)] if last else [vmem] * len(out_shape),
        scratch_shapes=scratch,
        input_output_aliases=aliases,
        compiler_params=pltpu.CompilerParams(vmem_limit_bytes=16 * MIB),
        cost_estimate=pl.CostEstimate(
            flops=2 * rows * sub * columns * len(parts),
            bytes_accessed=2 * sub * columns * len(parts),
            transcendentals=0,
        ),
    )(*operands)


def make_shards(n):
    order = ring_order(n)
    right = [(order[p], order[(p + 1) % n]) for p in range(n)]
    left = [(order[p], order[(p - 1) % n]) for p in range(n)]
    half = n // 2
    plan = [((half, 0), (half, 1))]
    for k in range(half - 1, 0, -1):
        plan += [((k, 1), (-k, 0)), ((k, 0), (-k, 1))]

    def shards(hidden, down_weight, residual, norm_gain, qkv_weight):
        rows, width = residual.shape
        sub = width // 2

        def send(x, pairs):
            return lax.ppermute(x, "tensor", pairs)

        *own, hidden = down(n, plan[0], hidden, down_weight, sub, first=True)
        arrived = [(send(own[0], right), send(own[1], left))]
        for step in range(1, n - 1, 2):
            own = down(n, [*plan[step], *plan[step + 1]], hidden, down_weight, sub)
            for i in range(2):
                up, down_ = own[2 * i : 2 * i + 2]
                if step + i > 1:
                    from_left, from_right = arrived[-2]
                    down_, hidden = add_step(down_, from_right, hidden)
                    up, hidden = add_step(up, from_left, hidden)
                arrived.append((send(up, right), send(down_, left)))
        own = down(n, [(0, 0), (0, 1)], hidden, down_weight, sub)
        (left_b, right_a), (left_a, right_b) = arrived[-2:]
        halves = [finish(0, own[0], residual, left_a, right_a), finish(1, own[1], residual, left_b, right_b)]

        gain = norm_gain[None, :]
        arrived = [(send(halves[0], right), send(halves[1], left))]
        arrived.append((send(halves[1], right), send(halves[0], left)))
        state, parts, xs = (), [], []
        for step in range(n - 1):
            x, y = arrived[step]
            k = step // 2 + 1
            parts += [(k, 1 - step % 2), (-k, step % 2)]
            xs += [y, x]
            if step in (n - 4, n - 5):
                arrived.append((send(x, right), send(y, left)))
            elif step == n - 3:
                state = qkv_step(n, parts, xs, gain, qkv_weight, state)
                *state, stream = qkv_step(n, [(0, 0), (0, 1)], halves, gain, qkv_weight, state, joins=True)
                parts, xs = [], []
            elif step == n - 2:
                state = qkv_step(n, parts[:1], xs[:1], gain, qkv_weight, state)
                (qkv,) = qkv_step(n, parts[1:], xs[1:], gain, qkv_weight, state, last=True)
            else:
                *state, x = qkv_step(n, parts, xs, gain, qkv_weight, state, hand_on=True)
                arrived.append((send(x, right), send(y, left)))
                parts, xs = [], []
        return stream, qkv

    return shards


def solution(mesh):
    in_specs = (P("dp", "tensor"), P("tensor", None), P("dp", "tensor"), P(), P(None, "tensor"))
    out_specs = (P("dp", "tensor"), P("dp", "tensor"))
    return jax.shard_map(
        make_shards(mesh.shape["tensor"]),
        mesh=mesh,
        in_specs=in_specs,
        out_specs=out_specs,
        check_vma=False,
    )
```

```python
import functools

import jax
import jax.numpy as jnp
from jax import lax
from jax.experimental import pallas as pl
from jax.experimental.pallas import tpu as pltpu
from jax.sharding import PartitionSpec as P

epsilon = 1e-05
f32, bf16 = jnp.float32, jnp.bfloat16
MIB = 1024 * 1024


def ring_order(n):
    return list(range(0, n, 2)) + list(range(n - 1, 0, -2))


def owner(n, offset):
    me = lax.axis_index("tensor")
    place = jnp.where(me % 2 == 0, me // 2, n - 1 - me // 2)
    place = (place + (offset + n)) % n
    return jnp.where(place < n // 2, 2 * place, 2 * (n - 1 - place) + 1)


def down_kernel(n, parts, x_ref, w_ref, *rest):
    outs, rest = rest[: len(parts)], list(rest[len(parts) :])
    buf, sems = rest[-2:]
    if len(rest) > 2:
        x_out, x_sem = rest[:2]
        x_copy = pltpu.make_async_copy(x_ref, x_out, x_sem)
        x_copy.start()
    else:
        x_out, x_copy = x_ref, None
    sub = outs[0].shape[1]
    per, (count, pieces) = sub // buf.shape[2], sems.shape
    tile, deep = buf.shape[2], buf.shape[1] // pieces

    def copies(i, begin, j):
        at = i * per + j
        columns = pl.ds(pl.multiple_of(begin + j * tile, tile), tile)
        for p in range(pieces):
            rows = pl.ds(p * deep, deep)
            yield pltpu.make_async_copy(w_ref.at[rows, columns], buf.at[at, rows], sems.at[at, p])

    begins = [owner(n, offset) * (2 * sub) + half * sub for offset, half in parts]
    for i in range(len(parts)):
        for j in range(per):
            for copy in copies(i, begins[i], j):
                copy.start()
    if x_copy is not None:
        x_copy.wait()
    for i, out in enumerate(outs):

        def step(j, carry):
            for copy in copies(i, begins[i], j):
                copy.wait()
            part = jnp.dot(x_out[...], buf[i * per + j], preferred_element_type=f32)
            out[:, pl.ds(pl.multiple_of(j * tile, tile), tile)] = part.astype(bf16)
            return carry

        lax.fori_loop(0, per, step, 0)


def down(n, parts, hidden, down_weight, sub, first=False):
    rows, inner = hidden.shape
    vmem, hbm = pl.BlockSpec(memory_space=pltpu.VMEM), pl.BlockSpec(memory_space=pltpu.HBM)
    pieces = max(p for p in (1, 2) if inner % (16 * p) == 0)
    tile = sub
    count = len(parts) * (sub // tile)
    weight = pltpu.with_memory_space_constraint(down_weight, pltpu.HBM)
    out_shape = [pltpu.VMEM((rows, sub), bf16)] * len(parts)
    scratch = [pltpu.VMEM((count, inner, tile), bf16), pltpu.SemaphoreType.DMA((count, pieces))]
    if first:
        hidden = pltpu.with_memory_space_constraint(hidden, pltpu.HBM)
        out_shape = out_shape + [pltpu.VMEM(hidden.shape, bf16)]
        scratch = [pltpu.SemaphoreType.DMA] + scratch
    return pl.pallas_call(
        functools.partial(down_kernel, n, parts),
        out_shape=out_shape,
        in_specs=[hbm if first else vmem, hbm],
        out_specs=[vmem] * len(out_shape),
        scratch_shapes=scratch,
        compiler_params=pltpu.CompilerParams(vmem_limit_bytes=14 * MIB),
        cost_estimate=pl.CostEstimate(
            flops=2 * rows * inner * sub * len(parts),
            bytes_accessed=2 * inner * sub * len(parts),
            transcendentals=0,
        ),
    )(hidden, weight)


def add_kernel(own_ref, x_ref, hidden_ref, out, hidden_out):
    out[...] = (own_ref[...].astype(f32) + x_ref[...].astype(f32)).astype(bf16)


def add_step(own, x, hidden):
    vmem = pl.BlockSpec(memory_space=pltpu.VMEM)
    return pl.pallas_call(
        add_kernel,
        out_shape=[pltpu.VMEM(x.shape, bf16), pltpu.VMEM(hidden.shape, bf16)],
        in_specs=[vmem] * 3,
        out_specs=[vmem] * 2,
        input_output_aliases={2: 1},
        compiler_params=pltpu.CompilerParams(vmem_limit_bytes=12 * MIB),
        cost_estimate=pl.CostEstimate(flops=x.size, bytes_accessed=6 * x.size, transcendentals=0),
    )(own, x, hidden)


def finish_kernel(half, own_ref, residual_ref, x_ref, y_ref, out):
    sub = out.shape[1]
    total = own_ref[...].astype(f32) + residual_ref[:, half * sub : (half + 1) * sub].astype(f32)
    out[...] = (total + x_ref[...].astype(f32) + y_ref[...].astype(f32)).astype(bf16)


def finish(half, own, residual, x, y):
    vmem = pl.BlockSpec(memory_space=pltpu.VMEM)
    return pl.pallas_call(
        functools.partial(finish_kernel, half),
        out_shape=[pltpu.VMEM(own.shape, bf16)],
        in_specs=[vmem] * 4,
        out_specs=[vmem],
        compiler_params=pltpu.CompilerParams(vmem_limit_bytes=12 * MIB),
        cost_estimate=pl.CostEstimate(flops=4 * own.size, bytes_accessed=10 * own.size, transcendentals=0),
    )(own, residual, x, y)[0]


def qkv_kernel(n, parts, first, last, joins, total_features, *refs):
    count = len(parts)
    xs, (gain_ref, w_ref), rest = refs[:count], refs[count : count + 2], refs[count + 2 :]
    sub = xs[0].shape[-1]
    if not first:
        total_in, squares_in, rest = rest[0], rest[1], rest[2:]
    if joins:
        for i, x_ref in enumerate(xs[-2:]):
            rest[2][:, i * sub : (i + 1) * sub] = x_ref[...]
    columns = w_ref.shape[1]
    scaled, rows_at = [], []
    squares = None if first else squares_in[...]
    for x_ref, (offset, half) in zip(xs, parts):
        row = pl.multiple_of(owner(n, offset) * (2 * sub) + half * sub, sub)
        x = x_ref[...].astype(f32)
        scaled.append((x * gain_ref[:, pl.ds(row, sub)]).astype(bf16))
        rows_at.append(row)
        for c in range(0, sub, 128):
            piece = x[:, c : c + 128]
            squares = piece * piece if squares is None else squares + piece * piece
    if last:
        mean = jnp.sum(squares, axis=1, keepdims=True) / total_features
        scale = jnp.sqrt(mean + epsilon)
        inverse = 1.0 / scale
    else:
        rest[1][...] = squares
    for c in range(0, columns, 256):
        wide = min(256, columns - c)
        acc = None if first else total_in[:, c : c + wide]
        for x, row in zip(scaled, rows_at):
            more = jnp.dot(x, w_ref[pl.ds(row, sub), c : c + wide], preferred_element_type=f32)
            acc = more if acc is None else acc + more
        if last:
            rest[0][:, c : c + wide] = (acc * inverse).astype(bf16)
        else:
            rest[0][:, c : c + wide] = acc


def qkv_step(n, parts, xs, gain, weight, state, last=False, hand_on=False, joins=False):
    rows, sub = xs[0].shape
    columns = weight.shape[1]
    vmem = pl.BlockSpec(memory_space=pltpu.VMEM)
    if last:
        out_shape = [jax.ShapeDtypeStruct((rows, columns), bf16)]
    else:
        out_shape = [pltpu.VMEM((rows, columns), f32), pltpu.VMEM((rows, 128), f32)]
    aliases = {}
    if joins:
        out_shape.append(jax.ShapeDtypeStruct((rows, 2 * sub), bf16))
    if hand_on:
        aliases = {len(xs) - 1: len(out_shape)}
        out_shape.append(pltpu.VMEM((rows, sub), bf16))
    operands = (*xs, gain, weight, *state)
    return pl.pallas_call(
        functools.partial(qkv_kernel, n, parts, not state, last, joins, float(weight.shape[0])),
        out_shape=out_shape,
        in_specs=[vmem] * len(operands),
        out_specs=[vmem] * len(out_shape),
        input_output_aliases=aliases,
        compiler_params=pltpu.CompilerParams(vmem_limit_bytes=16 * MIB),
        cost_estimate=pl.CostEstimate(
            flops=2 * rows * sub * columns * len(parts),
            bytes_accessed=2 * sub * columns * len(parts),
            transcendentals=0,
        ),
    )(*operands)


def make_shards(n):
    order = ring_order(n)
    right = [(order[p], order[(p + 1) % n]) for p in range(n)]
    left = [(order[p], order[(p - 1) % n]) for p in range(n)]
    half = n // 2
    plan = [((half, 0), (half, 1))]
    for k in range(half - 1, 0, -1):
        plan += [((k, 1), (-k, 0)), ((k, 0), (-k, 1))]

    def shards(hidden, down_weight, residual, norm_gain, qkv_weight):
        rows, width = residual.shape
        sub = width // 2

        def send(x, pairs):
            return lax.ppermute(x, "tensor", pairs)

        *own, hidden = down(n, plan[0], hidden, down_weight, sub, first=True)
        arrived = [(send(own[0], right), send(own[1], left))]
        for step in range(1, n - 1, 2):
            own = down(n, [*plan[step], *plan[step + 1]], hidden, down_weight, sub)
            for i in range(2):
                up, down_ = own[2 * i : 2 * i + 2]
                if step + i > 1:
                    from_left, from_right = arrived[-2]
                    down_, hidden = add_step(down_, from_right, hidden)
                    up, hidden = add_step(up, from_left, hidden)
                arrived.append((send(up, right), send(down_, left)))
        own = down(n, [(0, 0), (0, 1)], hidden, down_weight, sub)
        (left_b, right_a), (left_a, right_b) = arrived[-2:]
        halves = [finish(0, own[0], residual, left_a, right_a), finish(1, own[1], residual, left_b, right_b)]

        gain = norm_gain[None, :]
        arrived = [(send(halves[0], right), send(halves[1], left))]
        arrived.append((send(halves[1], right), send(halves[0], left)))
        state, parts, xs = (), [], []
        for step in range(n - 1):
            x, y = arrived[step]
            k = step // 2 + 1
            parts += [(k, 1 - step % 2), (-k, step % 2)]
            xs += [y, x]
            if step in (n - 4, n - 5, n - 7):
                arrived.append((send(x, right), send(y, left)))
            elif step == n - 3:
                state = qkv_step(n, parts, xs, gain, qkv_weight, state)
                *state, stream = qkv_step(n, [(0, 0), (0, 1)], halves, gain, qkv_weight, state, joins=True)
                parts, xs = [], []
            elif step == n - 2:
                state = qkv_step(n, parts[:1], xs[:1], gain, qkv_weight, state)
                (qkv,) = qkv_step(n, parts[1:], xs[1:], gain, qkv_weight, state, last=True)
            else:
                *state, x = qkv_step(n, parts, xs, gain, qkv_weight, state, hand_on=True)
                arrived.append((send(x, right), send(y, left)))
                parts, xs = [], []
        return stream, qkv

    return shards


def solution(mesh):
    in_specs = (P("dp", "tensor"), P("tensor", None), P("dp", "tensor"), P(), P(None, "tensor"))
    out_specs = (P("dp", "tensor"), P("dp", "tensor"))
    return jax.shard_map(
        make_shards(mesh.shape["tensor"]),
        mesh=mesh,
        in_specs=in_specs,
        out_specs=out_specs,
        check_vma=False,
    )
```
